1024 devices in a mesh: band: 128 (over x, z), sub: 8 (over y, core).
Axes of the slice: x: 4, y: 4, z: 32, core: 2. Of those that a mesh axis runs over, the one named last changes fastest.
Arguments:
- atmos_flux: bfloat16 [32, 1024, 1024], P(None, 'band', 'sub'), may hold values from -6 to 6
- weight_tiles: bfloat16 [128, 8, 32, 384, 128], P('band', 'sub'), may hold values from -0.3125 to 0.3125
- source_row: int32 [128, 8, 32], P('band', 'sub'), may hold values from 0 to 7
- target_code: int32 [128, 8, 32], P('band', 'sub'), may hold values from 0 to 127
- live_count: int32 [128, 8], P('band', 'sub'), may hold values from 8 to 32, as said below
Outputs:
- ocean_flux: float32 [32, 1048576], P(None, ('band', 'sub'))
The draws below stay inside these ranges and needn't reach their ends.
Inputs may be any that keep to these rules, and one draw needn't show every extreme that they name: `live_count`: each device has between 8 and 32 live entries; some device has exactly 32.
All inputs are finite; a program needn't handle non-finite values.
Results may differ from the reference program's by a relative error of at most 0.0036.
Values may be sent and summed in bfloat16 or wider, within the bound.
No kernel may reach another device: no remote copies, remote signals or barrier semaphores. Data moves between devices by JAX's collectives and lax.ppermute only.
A program may use at most 32 MiB of HBM per device.

```python
import jax
import jax.numpy as jnp
from jax import lax

FIELDS = 8
TIMES = 4
LON_DEV = 128
LAT_DEV = 8
OB_DEV = 8
OV_CAP = 32
LAT = 1024
LON = 1024
N_BAND = 128
N_SUB = 8


def draw_live_count(key, part):
    key = jax.random.fold_in(key, 7)
    first, second, third, fourth = jax.random.split(key, 4)
    shape = (N_BAND, N_SUB)
    inland = jax.random.randint(first, shape, OV_CAP // 4, OV_CAP // 2 + 1)
    coastal = jax.random.randint(second, shape, 3 * OV_CAP // 4, OV_CAP + 1)
    is_coast = jax.random.randint(third, shape, 0, 8) == 0
    counts = jnp.where(is_coast, coastal, inland).reshape(-1)
    chosen = jax.random.randint(fourth, (), 0, N_BAND * N_SUB)
    counts = jnp.where(jnp.arange(N_BAND * N_SUB) == chosen, OV_CAP, counts)
    return counts.reshape(shape).astype(jnp.int32)


def set_ends(values, rng, low, high):
    spot = [jax.random.randint(jax.random.fold_in(rng, axis), (), 0, length) for axis, length in enumerate(values.shape)]
    longest = values.shape.index(max(values.shape))
    next_to = spot[:longest] + [(spot[longest] + 1) % values.shape[longest]] + spot[longest + 1:]
    return values.at[tuple(spot)].set(low).at[tuple(next_to)].set(high)


def block_levels(key, extent, cuts, smallest, top_value):
    level = 1.0
    for position, parts in cuts:
        heights = jax.random.uniform(jax.random.fold_in(jax.random.fold_in(key, 6), position), (parts,), jnp.float32, smallest / len(cuts), top_value / len(cuts))
        level = level * jnp.repeat(jnp.exp(heights), extent[position] // parts).reshape((-1,) + (1,) * (len(extent) - 1 - position))
    return level


def centred(own_key, dims, scale, most, shards=(), kind=jnp.bfloat16):
    result = jax.random.normal(own_key, dims, jnp.float32) * scale
    if len(shards) > 0:
        result = block_levels(own_key, dims, shards, -0.22, 0.18) * result
    return jnp.clip(result, min=-most, max=most).astype(kind)


def setup_inputs(seed: int = 0) -> dict:
    keys = jax.random.split(jax.random.key(seed), 6)
    atmos_flux = centred(keys[0], (FIELDS * TIMES, LAT, LON), 1.0, 6.0, ((1, 128), (2, 8)))
    weight_tiles = centred(keys[1], (N_BAND, N_SUB, OV_CAP, 3 * LON_DEV, LON_DEV), (3 * LON_DEV) ** -0.5, 0.3125, ((0, 128), (1, 8)))
    source_row = set_ends(jax.random.randint(keys[2], (N_BAND, N_SUB, OV_CAP), 0, LAT_DEV), jax.random.fold_in(keys[2], 1), 0, LAT_DEV - 1).astype(jnp.int32)
    target_code = set_ends(jax.random.randint(keys[3], (N_BAND, N_SUB, OV_CAP), 0, 2 * N_SUB * OB_DEV), jax.random.fold_in(keys[3], 1), 0, (2 * N_SUB * OB_DEV) - 1).astype(jnp.int32)
    live_count = draw_live_count(jax.random.fold_in(keys[5], 71), 0)
    return dict(atmos_flux=atmos_flux, weight_tiles=weight_tiles, source_row=source_row, target_code=target_code, live_count=live_count)


def reference(atmos_flux, weight_tiles, source_row, target_code, live_count):
    fields = FIELDS * TIMES
    widened = jnp.pad(atmos_flux.astype(jnp.float32), ((0, 0), (1, 1), (1, 1)))
    grad_x = (0.5 * (widened[:, 1:-1, 2:] - widened[:, 1:-1, :-2])).astype(jnp.bfloat16)
    grad_y = (0.5 * (widened[:, 2:, 1:-1] - widened[:, :-2, 1:-1])).astype(jnp.bfloat16)

    def blocks(whole):
        shaped = whole.reshape(fields, N_BAND, LAT_DEV, N_SUB, LON_DEV)
        return shaped.transpose(1, 3, 2, 0, 4).reshape(N_BAND * N_SUB, LAT_DEV, fields, LON_DEV)

    operand = jnp.concatenate([blocks(atmos_flux), blocks(grad_x), blocks(grad_y)], axis=-1)
    targets = 2 * N_SUB * OB_DEV

    def one_device(items):
        rows_op, tiles_dev, rows_idx, codes, count_dev = items
        picked = rows_op[rows_idx]
        product = jnp.einsum("ekc,ecl->ekl", picked.astype(jnp.float32), tiles_dev.astype(jnp.float32), precision=lax.Precision.HIGHEST)
        live = (jnp.arange(OV_CAP, dtype=jnp.int32) < count_dev).astype(jnp.float32)
        selector = (codes[None, :] == jnp.arange(targets, dtype=jnp.int32)[:, None]).astype(jnp.float32) * live[None, :]
        summed = jnp.einsum("te,ekl->tkl", selector, product, precision=lax.Precision.HIGHEST)
        return summed.astype(jnp.bfloat16)

    partial_all = lax.map(one_device, (operand,
                                       weight_tiles.reshape(N_BAND * N_SUB, OV_CAP, 3 * LON_DEV, LON_DEV),
                                       source_row.reshape(N_BAND * N_SUB, OV_CAP),
                                       target_code.reshape(N_BAND * N_SUB, OV_CAP),
                                       live_count.reshape(N_BAND * N_SUB)))
    partial_all = partial_all.astype(jnp.float32).reshape(N_BAND, N_SUB, N_SUB, 2, OB_DEV, fields, LON_DEV)
    own_band = jnp.sum(partial_all[:, :, :, 0], axis=1)
    next_band = jnp.roll(jnp.sum(partial_all[:, :, :, 1], axis=1), 1, axis=0)
    total = own_band + next_band
    return total.transpose(3, 0, 1, 2, 4).reshape(fields, N_BAND * N_SUB * OB_DEV * LON_DEV)
```

```python
import jax
import jax.numpy as jnp
from jax import lax
from jax.experimental import pallas as pl
from jax.experimental.pallas import tpu as pltpu
from jax.sharding import PartitionSpec as P

OB_DEV = 8
LANES = 128
GROUP = 8
VMEM = pl.BlockSpec(memory_space=pltpu.VMEM)
SMEM = pl.BlockSpec(memory_space=pltpu.SMEM)


def swap_pairs(count, first):
    pairs = []
    for i in range(first, count - 1, 2):
        pairs += [(i, i + 1), (i + 1, i)]
    return pairs


def xor_pairs(count, mask):
    return [(i, i ^ mask) for i in range(count)]


def product_kernel(
    where_ref, row_ref, code_ref, live_ref, x_ref, pair_ref, beside_ref, next_ref, far_ref, w_ref,
    keep_ref, send_ref, away, xf, source,
):
    sub, band = where_ref[0], where_ref[1]
    fields, rows, width = x_ref.shape
    flat = fields * rows
    capacity = w_ref.shape[0]
    half = keep_ref.shape[0]
    keep_ref[...] = jnp.zeros_like(keep_ref)
    away[...] = jnp.zeros_like(away)

    def full(ref):
        return ref[...].astype(jnp.float32).reshape(flat, width)

    x, pair, beside, near, far = full(x_ref), full(pair_ref), full(beside_ref), full(next_ref), full(far_ref)
    odd_sub, odd_band = sub % 2 == 1, band % 2 == 1
    left, right = jnp.where(odd_sub, pair, beside), jnp.where(odd_sub, beside, pair)
    above, below = jnp.where(odd_band, near, far), jnp.where(odd_band, far, near)
    lane = lax.broadcasted_iota(jnp.int32, (flat, width), 1)
    later = pltpu.roll(jnp.where(lane == 0, right, x), width - 1, 1)
    earlier = pltpu.roll(jnp.where(lane == width - 1, left, x), 1, 1)
    grad_x = 0.5 * (later - earlier)
    xf[0] = x
    xf[1] = grad_x
    xf[2] = above
    xf[3] = below

    def row(which, r):
        return xf[which, pl.ds(r, fields, stride=rows), :]

    for r in range(rows):
        up = row(0, r - 1) if r > 0 else row(2, rows - 1)
        down = row(0, r + 1) if r < rows - 1 else row(3, 0)
        source[r, :, 0:width] = row(0, r).astype(jnp.bfloat16)
        source[r, :, width : 2 * width] = row(1, r).astype(jnp.bfloat16)
        source[r, :, 2 * width : 3 * width] = (0.5 * (down - up)).astype(jnp.bfloat16)

    live = live_ref[0]
    core, along = sub % 2, sub // 2
    for start in range(0, capacity, GROUP):

        @pl.when(start < live)
        def _(start=start):
            for e in range(start, start + GROUP):
                product = jnp.dot(source[row_ref[e]], w_ref[e], preferred_element_type=jnp.float32)
                product = jnp.where(e < live, product, 0.0)
                code = code_ref[e]
                dest = code // 16
                slot = ((dest // 2) ^ along) * 16 + code % 16
                mine = (dest % 2) == core

                @pl.when(mine)
                def _():
                    keep_ref[slot] += product

                @pl.when(jnp.logical_not(mine))
                def _():
                    away[slot] += product

    send_ref[...] = away[...].astype(jnp.bfloat16)


def pair_sum_kernel(keep_ref, got_ref, own_ref, *out_refs):
    count = own_ref.shape[0]
    own_ref[...] = keep_ref[0:count] + got_ref[0:count].astype(jnp.float32)
    for k, out in enumerate(out_refs, 1):
        span = slice(k * count, (k + 1) * count)
        out[...] = (keep_ref[span] + got_ref[span].astype(jnp.float32)).astype(jnp.bfloat16)


def total_kernel(own_ref, *refs):
    got, (here_ref, next_ref) = refs[:-2], refs[-2:]
    total = own_ref[...]
    for ref in got:
        total = total + ref[...].astype(jnp.float32)
    here_ref[...] = total[:OB_DEV]
    next_ref[...] = total[OB_DEV:].astype(jnp.bfloat16)


def final_kernel(here_ref, got_ref, out_ref):
    for q in range(OB_DEV):
        out_ref[:, q * LANES : (q + 1) * LANES] = here_ref[q] + got_ref[q].astype(jnp.float32)


def shards(atmos_flux, weight_tiles, source_row, target_code, live_count):
    fields, rows, width = atmos_flux.shape
    capacity = weight_tiles.shape[2]
    subs, bands = lax.axis_size("sub"), lax.axis_size("band")
    blocks = 2 * OB_DEV
    half = subs // 2 * blocks
    where = jnp.stack([lax.axis_index("sub"), lax.axis_index("band")]).astype(jnp.int32)
    beside = lax.ppermute(atmos_flux, "sub", swap_pairs(subs, 1))
    far = lax.ppermute(atmos_flux, "band", swap_pairs(bands, 1))
    pair = lax.ppermute(atmos_flux, "sub", swap_pairs(subs, 0))
    near = lax.ppermute(atmos_flux, "band", swap_pairs(bands, 0))
    keep, send = pl.pallas_call(
        product_kernel,
        out_shape=(
            jax.ShapeDtypeStruct((half, fields, width), jnp.float32),
            jax.ShapeDtypeStruct((half, fields, width), jnp.bfloat16),
        ),
        in_specs=[SMEM] * 4 + [VMEM] * 6,
        out_specs=(VMEM, VMEM),
        scratch_shapes=[
            pltpu.VMEM((half, fields, width), jnp.float32),
            pltpu.VMEM((4, fields * rows, width), jnp.float32),
            pltpu.VMEM((rows, fields, 3 * width), jnp.bfloat16),
        ],
        compiler_params=pltpu.CompilerParams(vmem_limit_bytes=24 * 2**20),
        name="product",
    )(
        where, source_row[0, 0], target_code[0, 0], live_count[0], atmos_flux, pair, beside, near, far,
        weight_tiles[0, 0],
    )
    got = lax.ppermute(send, "sub", xor_pairs(subs, 1))
    chunk = jax.ShapeDtypeStruct((blocks, fields, width), jnp.bfloat16)
    own, *outs = pl.pallas_call(
        pair_sum_kernel,
        out_shape=(jax.ShapeDtypeStruct(chunk.shape, jnp.float32),) + (chunk,) * (subs // 2 - 1),
        in_specs=[VMEM] * 2,
        out_specs=(VMEM,) * (subs // 2),
        compiler_params=pltpu.CompilerParams(vmem_limit_bytes=24 * 2**20),
        name="pair_sum",
    )(keep, got)
    arrived = [lax.ppermute(outs[k - 1], "sub", xor_pairs(subs, 2 * k)) for k in (2, 1, 3)]
    here, ahead = pl.pallas_call(
        total_kernel,
        out_shape=(
            jax.ShapeDtypeStruct((OB_DEV, fields, width), jnp.float32),
            jax.ShapeDtypeStruct((OB_DEV, fields, width), jnp.bfloat16),
        ),
        in_specs=[VMEM] * (subs // 2),
        out_specs=(VMEM, VMEM),
        compiler_params=pltpu.CompilerParams(vmem_limit_bytes=24 * 2**20),
        name="total",
    )(own, *arrived)
    behind = lax.ppermute(ahead, "band", [(i, (i + 1) % bands) for i in range(bands)])
    return pl.pallas_call(
        final_kernel,
        out_shape=jax.ShapeDtypeStruct((fields, OB_DEV * width), jnp.float32),
        in_specs=[VMEM] * 2,
        out_specs=VMEM,
        compiler_params=pltpu.CompilerParams(vmem_limit_bytes=24 * 2**20),
        name="final",
    )(here, behind)


def solution(mesh):
    return jax.shard_map(
        shards,
        mesh=mesh,
        in_specs=(
            P(None, "band", "sub"),
            P("band", "sub", None, None, None),
            P("band", "sub", None),
            P("band", "sub", None),
            P("band", "sub"),
        ),
        out_specs=P(None, ("band", "sub")),
        check_vma=False,
    )
```

```python
import jax
import jax.numpy as jnp
from jax import lax
from jax.experimental import pallas as pl
from jax.experimental.pallas import tpu as pltpu
from jax.sharding import PartitionSpec as P

OB_DEV = 8
LANES = 128
GROUP = 8
VMEM = pl.BlockSpec(memory_space=pltpu.VMEM)
SMEM = pl.BlockSpec(memory_space=pltpu.SMEM)


def swap_pairs(count, first):
    pairs = []
    for i in range(first, count - 1, 2):
        pairs += [(i, i + 1), (i + 1, i)]
    return pairs


def xor_pairs(count, mask):
    return [(i, i ^ mask) for i in range(count)]


def edge_kernel(x_ref, pair_ref, cross_ref):
    odd = lax.axis_index("band") % 2 == 1
    fields, rows, width = x_ref.shape
    x = x_ref[...].astype(jnp.float32)
    first, last = x[:, 0, :], x[:, rows - 1, :]
    pair_ref[...] = jnp.where(odd, first, last).astype(jnp.bfloat16)
    cross_ref[...] = jnp.where(odd, last, first).astype(jnp.bfloat16)


def entry(info_ref, e, live):
    core, along = lax.axis_index("sub") % 2, lax.axis_index("sub") // 2
    packed = info_ref[e]
    code = packed // 8
    dest = code // 16
    slot = ((dest % 2) ^ core) * 64 + ((dest // 2) ^ along) * 16 + code % 16
    return packed % 8, jnp.where(e < live, slot, 128)


def inner_kernel(info_ref, x_ref, w_hbm, acc_ref, w_ref, xf, source, sems):
    fields, rows, width = x_ref.shape
    flat = fields * rows
    capacity = w_ref.shape[0]
    live = info_ref[capacity]

    def load(start):
        span = pl.ds(start, GROUP)
        return pltpu.make_async_copy(w_hbm.at[span], w_ref.at[span], sems.at[start // GROUP])

    for start in range(0, capacity, GROUP):
        pl.when(start < live)(lambda start=start: load(start).start())
    acc_ref[...] = jnp.zeros_like(acc_ref)
    x = x_ref[...].astype(jnp.float32).reshape(flat, width)
    lane = lax.broadcasted_iota(jnp.int32, (flat, width), 1)
    later = pltpu.roll(jnp.where(lane == 0, 0.0, x), width - 1, 1)
    earlier = pltpu.roll(jnp.where(lane == width - 1, 0.0, x), 1, 1)
    xf[0] = x
    xf[1] = 0.5 * (later - earlier)

    def row(which, r):
        return xf[which, pl.ds(r, fields, stride=rows), :]

    for r in range(rows):
        up = row(0, r - 1) if r > 0 else 0.0
        down = row(0, r + 1) if r < rows - 1 else 0.0
        source[r, :, 0:width] = row(0, r).astype(jnp.bfloat16)
        source[r, :, width : 2 * width] = row(1, r).astype(jnp.bfloat16)
        source[r, :, 2 * width : 3 * width] = (0.5 * (down - up)).astype(jnp.bfloat16)

    for start in range(0, capacity, GROUP):

        @pl.when(start < live)
        def _(start=start):
            load(start).wait()
            for e in range(start, start + GROUP):
                r, slot = entry(info_ref, e, live)
                acc_ref[slot] += jnp.dot(source[r], w_ref[e], preferred_element_type=jnp.float32)


def border_kernel(info_ref, pair_ref, beside_ref, near_ref, far_ref, w_ref, acc_in, acc_ref, send_ref, xf, side, ends):
    del acc_in
    fields, rows, width = pair_ref.shape
    flat = fields * rows
    capacity = w_ref.shape[0]
    live = info_ref[capacity]
    odd_sub, odd_band = lax.axis_index("sub") % 2 == 1, lax.axis_index("band") % 2 == 1
    pair, beside = (ref[...].astype(jnp.float32).reshape(flat, width) for ref in (pair_ref, beside_ref))
    left = jnp.where(odd_sub, pair, beside)[:, width - 1 : width]
    right = jnp.where(odd_sub, beside, pair)[:, 0:1]
    xf[0] = jnp.broadcast_to(-0.5 * left, (flat, width))
    xf[1] = jnp.broadcast_to(0.5 * right, (flat, width))
    for r in range(rows):
        for which in range(2):
            side[which, r] = xf[which, pl.ds(r, fields, stride=rows), :]
    near, far = near_ref[...].astype(jnp.float32), far_ref[...].astype(jnp.float32)
    ends[...] = jnp.zeros_like(ends)
    ends[0] = (-0.5 * jnp.where(odd_band, near, far)).astype(jnp.bfloat16)
    ends[rows - 1] = (0.5 * jnp.where(odd_band, far, near)).astype(jnp.bfloat16)
    for start in range(0, capacity, GROUP):

        @pl.when(start < live)
        def _(start=start):
            for e in range(start, start + GROUP):
                r, slot = entry(info_ref, e, live)
                first = w_ref[e, width : width + 16, :].astype(jnp.float32)[0:1]
                last = w_ref[e, 2 * width - 16 : 2 * width, :].astype(jnp.float32)[15:16]
                acc_ref[slot] += (
                    jnp.dot(ends[r], w_ref[e, 2 * width : 3 * width, :], preferred_element_type=jnp.float32)
                    + side[0, r] * first
                    + side[1, r] * last
                )

    half = send_ref.shape[0]
    send_ref[...] = acc_ref[half : 2 * half].astype(jnp.bfloat16)


def pair_sum_kernel(keep_ref, got_ref, own_ref, *out_refs):
    count = own_ref.shape[0]
    own_ref[...] = keep_ref[0:count] + got_ref[0:count].astype(jnp.float32)
    for k, out in enumerate(out_refs, 1):
        span = slice(k * count, (k + 1) * count)
        out[...] = (keep_ref[span] + got_ref[span].astype(jnp.float32)).astype(jnp.bfloat16)


def total_kernel(own_ref, *refs):
    got, (here_ref, next_ref) = refs[:-2], refs[-2:]
    total = own_ref[...]
    for ref in got:
        total = total + ref[...].astype(jnp.float32)
    here_ref[...] = total[:OB_DEV]
    next_ref[...] = total[OB_DEV:].astype(jnp.bfloat16)


def final_kernel(here_ref, got_ref, out_ref):
    for q in range(OB_DEV):
        out_ref[:, q * LANES : (q + 1) * LANES] = here_ref[q] + got_ref[q].astype(jnp.float32)


def shards(atmos_flux, weight_tiles, source_row, target_code, live_count):
    fields, rows, width = atmos_flux.shape
    capacity = weight_tiles.shape[2]
    subs, bands = lax.axis_size("sub"), lax.axis_size("band")
    blocks = 2 * OB_DEV
    half = subs // 2 * blocks
    params = pltpu.CompilerParams(vmem_limit_bytes=24 * 2**20)
    info = jnp.concatenate([source_row[0, 0] + 8 * target_code[0, 0], live_count[0]])
    pair = lax.ppermute(atmos_flux, "sub", swap_pairs(subs, 0))
    beside = lax.ppermute(atmos_flux, "sub", swap_pairs(subs, 1))
    edge = jax.ShapeDtypeStruct((fields, width), jnp.bfloat16)
    pair_edge, cross_edge = pl.pallas_call(
        edge_kernel,
        out_shape=(edge, edge),
        in_specs=[VMEM],
        out_specs=(VMEM, VMEM),
        compiler_params=params,
        name="edges",
    )(atmos_flux)
    near = lax.ppermute(pair_edge, "band", swap_pairs(bands, 0))
    far = lax.ppermute(cross_edge, "band", swap_pairs(bands, 1))
    sums = jax.ShapeDtypeStruct((2 * half + 1, fields, width), jnp.float32)
    tiles = pltpu.with_memory_space_constraint(weight_tiles[0, 0], pltpu.HBM)
    acc, held = pl.pallas_call(
        inner_kernel,
        out_shape=(sums, jax.ShapeDtypeStruct(tiles.shape, tiles.dtype)),
        in_specs=[SMEM, VMEM, pl.BlockSpec(memory_space=pltpu.HBM)],
        out_specs=(VMEM, VMEM),
        scratch_shapes=[
            pltpu.VMEM((2, fields * rows, width), jnp.float32),
            pltpu.VMEM((rows, fields, 3 * width), jnp.bfloat16),
            pltpu.SemaphoreType.DMA((capacity // GROUP,)),
        ],
        compiler_params=params,
        cost_estimate=pl.CostEstimate(flops=100_000_000, bytes_accessed=6_000_000, transcendentals=0),
        name="inner",
    )(info, atmos_flux, tiles)
    acc, send = pl.pallas_call(
        border_kernel,
        out_shape=(sums, jax.ShapeDtypeStruct((half, fields, width), jnp.bfloat16)),
        in_specs=[SMEM] + [VMEM] * 6,
        out_specs=(VMEM, VMEM),
        scratch_shapes=[
            pltpu.VMEM((2, fields * rows, width), jnp.float32),
            pltpu.VMEM((2, rows, fields, width), jnp.float32),
            pltpu.VMEM((rows, fields, width), jnp.bfloat16),
        ],
        input_output_aliases={6: 0},
        compiler_params=params,
        name="border",
    )(info, pair, beside, near, far, held, acc)
    got = lax.ppermute(send, "sub", xor_pairs(subs, 1))
    chunk = jax.ShapeDtypeStruct((blocks, fields, width), jnp.bfloat16)
    own, *outs = pl.pallas_call(
        pair_sum_kernel,
        out_shape=(jax.ShapeDtypeStruct(chunk.shape, jnp.float32),) + (chunk,) * (subs // 2 - 1),
        in_specs=[VMEM] * 2,
        out_specs=(VMEM,) * (subs // 2),
        compiler_params=params,
        name="pair_sum",
    )(acc, got)
    arrived = [lax.ppermute(outs[k - 1], "sub", xor_pairs(subs, 2 * k)) for k in (2, 1, 3)]
    here, ahead = pl.pallas_call(
        total_kernel,
        out_shape=(
            jax.ShapeDtypeStruct((OB_DEV, fields, width), jnp.float32),
            jax.ShapeDtypeStruct((OB_DEV, fields, width), jnp.bfloat16),
        ),
        in_specs=[VMEM] * (subs // 2),
        out_specs=(VMEM, VMEM),
        compiler_params=params,
        name="total",
    )(own, *arrived)
    behind = lax.ppermute(ahead, "band", [(i, (i + 1) % bands) for i in range(bands)])
    return pl.pallas_call(
        final_kernel,
        out_shape=jax.ShapeDtypeStruct((fields, OB_DEV * width), jnp.float32),
        in_specs=[VMEM] * 2,
        out_specs=VMEM,
        compiler_params=params,
        name="final",
    )(here, behind)


def solution(mesh):
    return jax.shard_map(
        shards,
        mesh=mesh,
        in_specs=(
            P(None, "band", "sub"),
            P("band", "sub", None, None, None),
            P("band", "sub", None),
            P("band", "sub", None),
            P("band", "sub"),
        ),
        out_specs=P(None, ("band", "sub")),
        check_vma=False,
    )
```

```python
import jax
import jax.numpy as jnp
from jax import lax
from jax.experimental import pallas as pl
from jax.experimental.pallas import tpu as pltpu
from jax.sharding import PartitionSpec as P

OB_DEV = 8
LANES = 128
GROUP = 8
VMEM = pl.BlockSpec(memory_space=pltpu.VMEM)
SMEM = pl.BlockSpec(memory_space=pltpu.SMEM)
HBM = pl.BlockSpec(memory_space=pltpu.HBM)


def hbm(array):
    return pltpu.with_memory_space_constraint(array, pltpu.HBM)


def swap_pairs(count, first):
    pairs = []
    for i in range(first, count - 1, 2):
        pairs += [(i, i + 1), (i + 1, i)]
    return pairs


def xor_pairs(count, mask):
    return [(i, i ^ mask) for i in range(count)]


def index_copies(refs, scratch, sems):
    return [pltpu.make_async_copy(ref, to, sems.at[i]) for i, (ref, to) in enumerate(zip(refs, scratch))]


def entry(row_ref, code_ref, e, live):
    core, along = lax.axis_index("sub") % 2, lax.axis_index("sub") // 2
    code = code_ref[0, 0, e]
    dest = code // 16
    slot = ((dest % 2) ^ core) * 64 + ((dest // 2) ^ along) * 16 + code % 16
    return row_ref[0, 0, e], jnp.where(e < live, slot, 128)


def inner_kernel(
    row_hbm, code_hbm, live_ref, x_hbm, w_hbm, acc_ref, w_ref,
    row_ref, code_ref, x_ref, xf, source, index_sems, x_sem, sems,
):
    fields, rows, width = x_ref.shape
    flat = fields * rows
    capacity = w_ref.shape[0]
    indices = index_copies((row_hbm, code_hbm), (row_ref, code_ref), index_sems)
    x_copy = pltpu.make_async_copy(x_hbm, x_ref, x_sem)

    def load(start):
        span = pl.ds(start, GROUP)
        return pltpu.make_async_copy(w_hbm.at[span], w_ref.at[span], sems.at[start // GROUP])

    for copy in indices:
        copy.start()
    x_copy.start()
    load(0).start()
    acc_ref[...] = jnp.zeros_like(acc_ref)
    for copy in indices:
        copy.wait()
    live = live_ref[0, 0]
    for start in range(GROUP, capacity, GROUP):
        pl.when(start < live)(lambda start=start: load(start).start())
    x_copy.wait()
    x = x_ref[...].astype(jnp.float32).reshape(flat, width)
    lane = lax.broadcasted_iota(jnp.int32, (flat, width), 1)
    later = pltpu.roll(jnp.where(lane == 0, 0.0, x), width - 1, 1)
    earlier = pltpu.roll(jnp.where(lane == width - 1, 0.0, x), 1, 1)
    xf[0] = x
    xf[1] = 0.5 * (later - earlier)

    def row(which, r):
        return xf[which, pl.ds(r, fields, stride=rows), :]

    for r in range(rows):
        up = row(0, r - 1) if r > 0 else 0.0
        down = row(0, r + 1) if r < rows - 1 else 0.0
        source[r, :, 0:width] = row(0, r).astype(jnp.bfloat16)
        source[r, :, width : 2 * width] = row(1, r).astype(jnp.bfloat16)
        source[r, :, 2 * width : 3 * width] = (0.5 * (down - up)).astype(jnp.bfloat16)

    def accumulate(start):
        load(start).wait()
        for e in range(start, start + GROUP):
            r, slot = entry(row_ref, code_ref, e, live)
            acc_ref[slot] += jnp.dot(source[r], w_ref[e], preferred_element_type=jnp.float32)

    accumulate(0)
    for start in range(GROUP, capacity, GROUP):
        pl.when(start < live)(lambda start=start: accumulate(start))


def border_kernel(
    row_hbm, code_hbm, live_ref, beside_ref, near_ref, far_ref, pair_ref, w_ref, acc_in, acc_ref, send_ref,
    row_ref, code_ref, xf, side, ends, index_sems,
):
    del acc_in
    fields, rows, width = pair_ref.shape
    flat = fields * rows
    capacity = w_ref.shape[0]
    indices = index_copies((row_hbm, code_hbm), (row_ref, code_ref), index_sems)
    for copy in indices:
        copy.start()
    odd_sub, odd_band = lax.axis_index("sub") % 2 == 1, lax.axis_index("band") % 2 == 1
    pair, beside, near, far = (
        ref[...].astype(jnp.float32).reshape(flat, width) for ref in (pair_ref, beside_ref, near_ref, far_ref)
    )
    left = jnp.where(odd_sub, pair, beside)[:, width - 1 : width]
    right = jnp.where(odd_sub, beside, pair)[:, 0:1]
    xf[0] = jnp.broadcast_to(-0.5 * left, (flat, width))
    xf[1] = jnp.broadcast_to(0.5 * right, (flat, width))
    xf[2] = -0.5 * jnp.where(odd_band, near, far)
    xf[3] = 0.5 * jnp.where(odd_band, far, near)

    def row(which, r):
        return xf[which, pl.ds(r, fields, stride=rows), :]

    for r in range(rows):
        for which in range(2):
            side[which, r] = row(which, r)
    ends[...] = jnp.zeros_like(ends)
    ends[0] = row(2, rows - 1).astype(jnp.bfloat16)
    ends[rows - 1] = row(3, 0).astype(jnp.bfloat16)
    for copy in indices:
        copy.wait()
    live = live_ref[0, 0]

    def accumulate(start):
        for e in range(start, start + GROUP):
            r, slot = entry(row_ref, code_ref, e, live)
            first = w_ref[e, width : width + 16, :].astype(jnp.float32)[0:1]
            last = w_ref[e, 2 * width - 16 : 2 * width, :].astype(jnp.float32)[15:16]
            acc_ref[slot] += (
                jnp.dot(ends[r], w_ref[e, 2 * width : 3 * width, :], preferred_element_type=jnp.float32)
                + side[0, r] * first
                + side[1, r] * last
            )

    accumulate(0)
    for start in range(GROUP, capacity, GROUP):
        pl.when(start < live)(lambda start=start: accumulate(start))
    half = send_ref.shape[0]
    send_ref[...] = acc_ref[half : 2 * half].astype(jnp.bfloat16)


def pair_sum_kernel(keep_ref, got_ref, own_ref, out_ref):
    along = lax.axis_index("sub") // 2
    chips, count = out_ref.shape[:2]
    for k in range(chips):
        span = slice(k * count, (k + 1) * count)
        out_ref[along ^ k] = (keep_ref[span] + got_ref[span].astype(jnp.float32)).astype(jnp.bfloat16)
    own_ref[...] = keep_ref[0:count] + got_ref[0:count].astype(jnp.float32)


def total_kernel(own_ref, got_ref, here_ref, next_ref):
    along = lax.axis_index("sub") // 2
    total = own_ref[...]
    for k in range(1, got_ref.shape[0]):
        total = total + got_ref[along ^ k].astype(jnp.float32)
    here_ref[...] = total[:OB_DEV]
    next_ref[...] = total[OB_DEV:].astype(jnp.bfloat16)


def final_kernel(here_ref, got_ref, out_ref):
    for q in range(OB_DEV):
        out_ref[:, q * LANES : (q + 1) * LANES] = here_ref[q] + got_ref[q].astype(jnp.float32)


def shards(atmos_flux, weight_tiles, source_row, target_code, live_count):
    fields, rows, width = atmos_flux.shape
    capacity = weight_tiles.shape[2]
    subs, bands = lax.axis_size("sub"), lax.axis_size("band")
    blocks = 2 * OB_DEV
    half = subs // 2 * blocks
    params = pltpu.CompilerParams(vmem_limit_bytes=24 * 2**20)
    far = lax.ppermute(atmos_flux, "band", swap_pairs(bands, 1))
    beside = lax.ppermute(atmos_flux, "sub", swap_pairs(subs, 1))
    pair = lax.ppermute(atmos_flux, "sub", swap_pairs(subs, 0))
    near = lax.ppermute(atmos_flux, "band", swap_pairs(bands, 0))
    sums = jax.ShapeDtypeStruct((2 * half + 1, fields, width), jnp.float32)
    indices = (hbm(source_row), hbm(target_code))
    index_scratch = [pltpu.SMEM(a.shape, a.dtype) for a in indices]
    tiles = hbm(weight_tiles[0, 0])
    acc, held = pl.pallas_call(
        inner_kernel,
        out_shape=(sums, jax.ShapeDtypeStruct(tiles.shape, tiles.dtype)),
        in_specs=[HBM, HBM, SMEM, HBM, HBM],
        out_specs=(VMEM, VMEM),
        scratch_shapes=index_scratch + [
            pltpu.VMEM((fields, rows, width), atmos_flux.dtype),
            pltpu.VMEM((2, fields * rows, width), jnp.float32),
            pltpu.VMEM((rows, fields, 3 * width), jnp.bfloat16),
            pltpu.SemaphoreType.DMA((2,)),
            pltpu.SemaphoreType.DMA,
            pltpu.SemaphoreType.DMA((capacity // GROUP,)),
        ],
        compiler_params=params,
        cost_estimate=pl.CostEstimate(flops=100_000_000, bytes_accessed=6_000_000, transcendentals=0),
        name="inner",
    )(*indices, live_count, hbm(atmos_flux), tiles)
    acc, send = pl.pallas_call(
        border_kernel,
        out_shape=(sums, jax.ShapeDtypeStruct((half, fields, width), jnp.bfloat16)),
        in_specs=[HBM, HBM, SMEM] + [VMEM] * 6,
        out_specs=(VMEM, VMEM),
        scratch_shapes=index_scratch + [
            pltpu.VMEM((4, fields * rows, width), jnp.float32),
            pltpu.VMEM((2, rows, fields, width), jnp.float32),
            pltpu.VMEM((rows, fields, width), jnp.bfloat16),
            pltpu.SemaphoreType.DMA((2,)),
        ],
        input_output_aliases={8: 0},
        compiler_params=params,
        name="border",
    )(*indices, live_count, beside, near, far, pair, held, acc)
    got = lax.ppermute(send, "sub", xor_pairs(subs, 1))
    own, outs = pl.pallas_call(
        pair_sum_kernel,
        out_shape=(
            jax.ShapeDtypeStruct((blocks, fields, width), jnp.float32),
            jax.ShapeDtypeStruct((subs // 2, blocks, fields, width), jnp.bfloat16),
        ),
        in_specs=[VMEM] * 2,
        out_specs=(VMEM, VMEM),
        compiler_params=params,
        name="pair_sum",
    )(acc, got)
    groups = [list(range(core, subs, 2)) for core in range(2)]
    arrived = lax.all_to_all(outs, "sub", split_axis=0, concat_axis=0, axis_index_groups=groups, tiled=True)
    here, ahead = pl.pallas_call(
        total_kernel,
        out_shape=(
            jax.ShapeDtypeStruct((OB_DEV, fields, width), jnp.float32),
            jax.ShapeDtypeStruct((OB_DEV, fields, width), jnp.bfloat16),
        ),
        in_specs=[VMEM] * 2,
        out_specs=(VMEM, VMEM),
        compiler_params=params,
        name="total",
    )(own, arrived)
    behind = lax.ppermute(ahead, "band", [(i, (i + 1) % bands) for i in range(bands)])
    return pl.pallas_call(
        final_kernel,
        out_shape=jax.ShapeDtypeStruct((fields, OB_DEV * width), jnp.float32),
        in_specs=[VMEM] * 2,
        out_specs=VMEM,
        compiler_params=params,
        name="final",
    )(here, behind)


def solution(mesh):
    return jax.shard_map(
        shards,
        mesh=mesh,
        in_specs=(
            P(None, "band", "sub"),
            P("band", "sub", None, None, None),
            P("band", "sub", None),
            P("band", "sub", None),
            P("band", "sub"),
        ),
        out_specs=P(None, ("band", "sub")),
        check_vma=False,
    )
```

```python
import jax
import jax.numpy as jnp
from jax import lax
from jax.experimental import pallas as pl
from jax.experimental.pallas import tpu as pltpu
from jax.sharding import PartitionSpec as P

OB_DEV = 8
PLANE = 32
OUTER = 64
LANES = 128
GROUP = 8
VMEM = pl.BlockSpec(memory_space=pltpu.VMEM)
SMEM = pl.BlockSpec(memory_space=pltpu.SMEM)
HBM = pl.BlockSpec(memory_space=pltpu.HBM)


def hbm(array):
    return pltpu.with_memory_space_constraint(array, pltpu.HBM)


def swap_pairs(count, first):
    pairs = []
    for i in range(first, count - 1, 2):
        pairs += [(i, i + 1), (i + 1, i)]
    return pairs


def xor_pairs(count, mask):
    return [(i, i ^ mask) for i in range(count)]


def index_copies(refs, scratch, sems):
    return [pltpu.make_async_copy(ref, to, sems.at[i]) for i, (ref, to) in enumerate(zip(refs, scratch))]


def entry(row_ref, code_ref, e, live):
    core, along = lax.axis_index("sub") % 2, lax.axis_index("sub") // 2
    code = code_ref[0, 0, e]
    dest = code // 16
    slot = ((dest % 2) ^ core) * 64 + ((dest // 2) ^ along) * 16 + code % 16
    return row_ref[0, 0, e], jnp.where(e < live, slot, 128)


def edge_rows(w_ref, e, width, right_first):
    right = w_ref[e, 2 * width - 16 : 2 * width, :].astype(jnp.float32)[15:16]
    left = w_ref[e, width : width + 16, :].astype(jnp.float32)[0:1]
    return jnp.where(right_first, right, left), jnp.where(right_first, left, right)


def column_block(rows, last, offset):
    place = lax.broadcasted_iota(jnp.int32, rows[0].shape, 1)
    block = jnp.zeros_like(rows[0])
    for r, values in enumerate(rows):
        block = jnp.where(place == offset + r, jnp.where(last, values[:, -1:], values[:, 0:1]), block)
    return block


def inner_kernel(
    row_hbm, code_hbm, live_ref, x_hbm, w_hbm, acc_ref, w_ref, meta_ref,
    row_ref, code_ref, row_lanes, code_lanes, x_ref, xf, source, edge, index_sems, x_sem, sems,
):
    fields, rows, width = x_ref.shape
    flat = fields * rows
    capacity = w_ref.shape[0]
    core, along = lax.axis_index("sub") % 2, lax.axis_index("sub") // 2
    indices = index_copies(
        (row_hbm, code_hbm, row_hbm, code_hbm), (row_ref, code_ref, row_lanes, code_lanes), index_sems
    )
    x_copy = pltpu.make_async_copy(x_hbm, x_ref, x_sem)

    def load(start):
        span = pl.ds(start, GROUP)
        return pltpu.make_async_copy(w_hbm.at[span], w_ref.at[span], sems.at[start // GROUP])

    live = live_ref[0, 0]
    for copy in indices:
        copy.start()
    x_copy.start()
    load(0).start()
    for start in range(GROUP, capacity, GROUP):
        pl.when(start < live)(lambda start=start: load(start).start())
    acc_ref[...] = jnp.zeros_like(acc_ref)
    edge[...] = jnp.zeros_like(edge)
    for copy in indices:
        copy.wait()
    x_copy.wait()
    x = x_ref[...].astype(jnp.float32).reshape(flat, width)
    lane = lax.broadcasted_iota(jnp.int32, (flat, width), 1)
    later = pltpu.roll(jnp.where(lane == 0, 0.0, x), width - 1, 1)
    earlier = pltpu.roll(jnp.where(lane == width - 1, 0.0, x), 1, 1)
    xf[0] = x
    xf[1] = 0.5 * (later - earlier)

    def row(which, r):
        return xf[which, pl.ds(r, fields, stride=rows), :]

    for r in range(rows):
        up = row(0, r - 1) if r > 0 else 0.0
        down = row(0, r + 1) if r < rows - 1 else 0.0
        source[r, :, 0:width] = row(0, r).astype(jnp.bfloat16)
        source[r, :, width : 2 * width] = row(1, r).astype(jnp.bfloat16)
        source[r, :, 2 * width : 3 * width] = (0.5 * (down - up)).astype(jnp.bfloat16)

    def accumulate(start):
        load(start).wait()
        for e in range(start, start + GROUP):
            to_mate, to_side = edge_rows(w_ref, e, width, core == 0)
            edge[0, e : e + 1] = to_mate
            edge[1, e : e + 1] = to_side
        places = [entry(row_ref, code_ref, e, live) for e in range(start, start + GROUP)]
        products = [
            jnp.dot(source[r], w_ref[start + i], preferred_element_type=jnp.float32) for i, (r, _) in enumerate(places)
        ]
        for (_, slot), product in zip(places, products):
            acc_ref[slot] += product

    accumulate(0)
    for start in range(GROUP, capacity, GROUP):
        pl.when(start < live)(lambda start=start: accumulate(start))
    meta_ref[0] = edge[0].astype(jnp.bfloat16)
    meta_ref[3] = edge[1].astype(jnp.bfloat16)
    columns = [row(0, r) for r in range(rows)]
    meta_ref[1] = column_block(columns, core == 0, 0).astype(jnp.bfloat16)
    meta_ref[4] = column_block(columns, core == 1, OUTER + core * rows).astype(jnp.bfloat16)
    code = code_lanes[0]
    dest = code // 16
    slot = ((dest % 2) ^ core) * 64 + ((dest // 2) ^ along) * 16 + code % 16
    alive = lax.broadcasted_iota(jnp.int32, slot.shape, 1) < live
    slot = jnp.where(alive, slot, 128)
    code = jnp.where(alive, code, 255)
    edge[0] = jnp.zeros_like(edge[0])
    edge[0, 0:1, 0:capacity] = row_lanes[0].astype(jnp.float32)
    edge[0, 1:2, 0:capacity] = slot.astype(jnp.float32)
    edge[0, 2:3, 0:capacity] = code.astype(jnp.float32)
    meta_ref[2] = edge[0].astype(jnp.bfloat16)


def border_kernel(
    row_hbm, code_hbm, live_ref, far_ref, first_ref, near_ref, w_ref, meta_ref, acc_in, acc_ref, send_ref,
    row_ref, code_ref, xf, ends, index_sems,
):
    del acc_in
    fields, rows, width = near_ref.shape
    flat = fields * rows
    capacity = w_ref.shape[0]
    indices = index_copies((row_hbm, code_hbm), (row_ref, code_ref), index_sems)
    for copy in indices:
        copy.start()
    odd_band = lax.axis_index("band") % 2 == 1
    near, first, far = (
        ref[...].astype(jnp.float32).reshape(flat, width) for ref in (near_ref, first_ref, far_ref)
    )
    near = near + first
    xf[0] = -0.5 * jnp.where(odd_band, near, far)
    xf[1] = 0.5 * jnp.where(odd_band, far, near)
    ends[...] = jnp.zeros_like(ends)
    ends[0] = xf[0, pl.ds(rows - 1, fields, stride=rows), :].astype(jnp.bfloat16)
    ends[rows - 1] = xf[1, pl.ds(0, fields, stride=rows), :].astype(jnp.bfloat16)
    for copy in indices:
        copy.wait()
    live = live_ref[0, 0]

    def accumulate(start):
        places = [entry(row_ref, code_ref, e, live) for e in range(start, start + GROUP)]
        products = [
            jnp.dot(ends[r], w_ref[start + i, 2 * width : 3 * width, :], preferred_element_type=jnp.float32)
            for i, (r, _) in enumerate(places)
        ]
        for (_, slot), product in zip(places, products):
            acc_ref[slot] += product

    accumulate(0)
    for start in range(GROUP, capacity, GROUP):
        pl.when(start < live)(lambda start=start: accumulate(start))
    extra = meta_ref.shape[0]
    half = send_ref.shape[0] - extra
    send_ref[0:half] = acc_ref[half : 2 * half].astype(jnp.bfloat16)
    send_ref[half : half + extra] = meta_ref[...]


def pair_sum_kernel(keep_ref, sent_ref, got_ref, own_ref, out_ref, select, edges):
    core, along = lax.axis_index("sub") % 2, lax.axis_index("sub") // 2
    count, fields, width = own_ref.shape
    chips = out_ref.shape[0]
    half = chips * count
    lane = lax.broadcasted_iota(jnp.int32, (1, width), 1)
    mine, theirs = sent_ref[half + 2].astype(jnp.float32), got_ref[half + 2].astype(jnp.float32)
    rolled = pltpu.roll(theirs, fields, 1)
    rows = jnp.where(lane < fields, mine[0:1], rolled[0:1])
    slots = jnp.where(lane < fields, mine[1:2], rolled[1:2] - half)
    place = lax.broadcasted_iota(jnp.int32, (width, width), 0).astype(jnp.float32)
    part = lax.broadcasted_iota(jnp.int32, (width, width), 1) // fields
    sign = jnp.where(core == 0, 0.5, -0.5)
    columns = jnp.zeros((fields, width), jnp.float32)
    for k, (block, factor) in enumerate(zip((got_ref[half + 1], sent_ref[half + 1]), (sign, -sign))):
        pick = jnp.where((place == rows) & (part == k), factor, 0.0).astype(jnp.bfloat16)
        columns = columns + jnp.dot(block, pick, preferred_element_type=jnp.float32)
    for t in range(half):
        select[t * fields : (t + 1) * fields] = jnp.where(slots == t, columns, 0.0).astype(jnp.bfloat16)
    edges[...] = jnp.zeros_like(edges)
    edges[0:fields] = sent_ref[half]
    edges[fields : 2 * fields] = got_ref[half]
    for k in range(chips):
        span = slice(k * count, (k + 1) * count)
        border = jnp.dot(
            select[k * count * fields : (k + 1) * count * fields], edges[...], preferred_element_type=jnp.float32
        )
        total = keep_ref[span] + got_ref[span].astype(jnp.float32) + border.reshape(count, fields, width)
        if k == 0:
            own_ref[...] = total
        out_ref[along ^ k, 0:count] = total.astype(jnp.bfloat16)
    first = core == 0
    outer = sent_ref[half + 4] + got_ref[half + 4]
    vectors = jnp.where(
        lax.broadcasted_iota(jnp.int32, mine.shape, 0) < 8,
        jnp.where(first, mine, theirs),
        pltpu.roll(jnp.where(first, theirs, mine), 8, 0),
    ).astype(jnp.bfloat16) + outer
    sides = [jnp.where(first == (k == 0), sent_ref[half + 3], got_ref[half + 3]) for k in range(2)]
    for k in range(chips):
        for i, block in enumerate((*sides, vectors)):
            out_ref[k, count + i] = block


def total_kernel(own_ref, got_ref, here_ref, next_ref, select, edges):
    sub = lax.axis_index("sub")
    along = sub // 2
    count, fields, width = own_ref.shape
    chips, rows = got_ref.shape[0], 8
    sets = width // fields
    lane = lax.broadcasted_iota(jnp.int32, (1, width), 1)
    place = lax.broadcasted_iota(jnp.int32, (width, width), 0).astype(jnp.float32)
    total = own_ref[...]
    for k in range(1, chips):
        total = total + got_ref[along ^ k, 0:count].astype(jnp.float32)
    for group in range(2 * chips // sets):
        columns = jnp.zeros((fields, width), jnp.float32)
        targets = jnp.full((1, width), -1.0, jnp.float32)
        for i in range(sets):
            chip, core = divmod(group * sets + i, 2)
            edges[group, i * fields : (i + 1) * fields] = got_ref[chip, count + core]
            vectors = got_ref[chip, count + 2].astype(jnp.float32)
            if i:
                vectors = pltpu.roll(vectors, i * fields, 1)
            inside = (lane >= i * fields) & (lane < (i + 1) * fields)
            targets = jnp.where(inside, vectors[8 * core + 2 : 8 * core + 3], targets)
            beside = chip + 2 * core - 1
            if 0 <= beside < chips:
                source = vectors[8 * core : 8 * core + 1] + (OUTER if core else OUTER + rows)
                pick = jnp.where((place == source) & inside, 0.5 if core else -0.5, 0.0).astype(jnp.bfloat16)
                columns = columns + jnp.dot(got_ref[beside, count + 2], pick, preferred_element_type=jnp.float32)
        targets = targets - (sub * count).astype(jnp.float32)
        for t in range(count):
            select[t * fields : (t + 1) * fields] = jnp.where(targets == t, columns, 0.0).astype(jnp.bfloat16)
        border = jnp.dot(select[...], edges[group], preferred_element_type=jnp.float32)
        total = total + border.reshape(count, fields, width)
    here_ref[...] = total[:OB_DEV]
    next_ref[...] = total[OB_DEV:].astype(jnp.bfloat16)


def final_kernel(here_ref, got_ref, out_ref):
    for q in range(OB_DEV):
        out_ref[:, q * LANES : (q + 1) * LANES] = here_ref[q] + got_ref[q].astype(jnp.float32)


def shards(atmos_flux, weight_tiles, source_row, target_code, live_count):
    fields, rows, width = atmos_flux.shape
    capacity = weight_tiles.shape[2]
    subs, bands = lax.axis_size("sub"), lax.axis_size("band")
    blocks = 2 * OB_DEV
    half = subs // 2 * blocks
    params = pltpu.CompilerParams(vmem_limit_bytes=24 * 2**20)
    far = lax.ppermute(atmos_flux, "band", swap_pairs(bands, 1))
    pairs = swap_pairs(bands, 0)
    first = lax.ppermute(atmos_flux, "band", [p for p in pairs if min(p) % PLANE == 0])
    near = lax.ppermute(atmos_flux, "band", [p for p in pairs if min(p) % PLANE != 0])
    sums = jax.ShapeDtypeStruct((2 * half + 1, fields, width), jnp.float32)
    indices = (hbm(source_row), hbm(target_code))
    index_scratch = [pltpu.SMEM(a.shape, a.dtype) for a in indices]
    tiles = hbm(weight_tiles[0, 0])
    meta = jax.ShapeDtypeStruct((5, fields, width), jnp.bfloat16)
    acc, held, meta = pl.pallas_call(
        inner_kernel,
        out_shape=(sums, jax.ShapeDtypeStruct(tiles.shape, tiles.dtype), meta),
        in_specs=[HBM, HBM, SMEM, HBM, HBM],
        out_specs=(VMEM, VMEM, VMEM),
        scratch_shapes=index_scratch + [pltpu.VMEM(a.shape, a.dtype) for a in indices] + [
            pltpu.VMEM((fields, rows, width), atmos_flux.dtype),
            pltpu.VMEM((2, fields * rows, width), jnp.float32),
            pltpu.VMEM((rows, fields, 3 * width), jnp.bfloat16),
            pltpu.VMEM((2, capacity, width), jnp.float32),
            pltpu.SemaphoreType.DMA((4,)),
            pltpu.SemaphoreType.DMA,
            pltpu.SemaphoreType.DMA((capacity // GROUP,)),
        ],
        compiler_params=params,
        cost_estimate=pl.CostEstimate(flops=100_000_000, bytes_accessed=6_000_000, transcendentals=0),
        name="inner",
    )(*indices, live_count, hbm(atmos_flux), tiles)
    payload = jax.ShapeDtypeStruct((half + 5, fields, width), jnp.bfloat16)
    acc, send = pl.pallas_call(
        border_kernel,
        out_shape=(sums, payload),
        in_specs=[HBM, HBM, SMEM] + [VMEM] * 6,
        out_specs=(VMEM, VMEM),
        scratch_shapes=index_scratch + [
            pltpu.VMEM((2, fields * rows, width), jnp.float32),
            pltpu.VMEM((rows, fields, width), jnp.bfloat16),
            pltpu.SemaphoreType.DMA((2,)),
        ],
        input_output_aliases={8: 0},
        compiler_params=params,
        cost_estimate=pl.CostEstimate(flops=30_000_000, bytes_accessed=4_000_000, transcendentals=0),
        name="border",
    )(*indices, live_count, far, first, near, held, meta, acc)
    got = lax.ppermute(send, "sub", xor_pairs(subs, 1))
    own, outs = pl.pallas_call(
        pair_sum_kernel,
        out_shape=(
            jax.ShapeDtypeStruct((blocks, fields, width), jnp.float32),
            jax.ShapeDtypeStruct((subs // 2, blocks + 3, fields, width), jnp.bfloat16),
        ),
        in_specs=[VMEM] * 3,
        out_specs=(VMEM, VMEM),
        scratch_shapes=[
            pltpu.VMEM((half * fields, width), jnp.bfloat16),
            pltpu.VMEM((width, width), jnp.bfloat16),
        ],
        compiler_params=params,
        name="pair_sum",
    )(acc, send, got)
    groups = [list(range(core, subs, 2)) for core in range(2)]
    arrived = lax.all_to_all(outs, "sub", split_axis=0, concat_axis=0, axis_index_groups=groups, tiled=True)
    here, ahead = pl.pallas_call(
        total_kernel,
        out_shape=(
            jax.ShapeDtypeStruct((OB_DEV, fields, width), jnp.float32),
            jax.ShapeDtypeStruct((OB_DEV, fields, width), jnp.bfloat16),
        ),
        in_specs=[VMEM] * 2,
        out_specs=(VMEM, VMEM),
        scratch_shapes=[
            pltpu.VMEM((blocks * fields, width), jnp.bfloat16),
            pltpu.VMEM((subs * fields // width, width, width), jnp.bfloat16),
        ],
        compiler_params=params,
        name="total",
    )(own, arrived)
    behind = lax.ppermute(ahead, "band", [(i, (i + 1) % bands) for i in range(bands)])
    return pl.pallas_call(
        final_kernel,
        out_shape=jax.ShapeDtypeStruct((fields, OB_DEV * width), jnp.float32),
        in_specs=[VMEM] * 2,
        out_specs=VMEM,
        compiler_params=params,
        name="final",
    )(here, behind)


def solution(mesh):
    return jax.shard_map(
        shards,
        mesh=mesh,
        in_specs=(
            P(None, "band", "sub"),
            P("band", "sub", None, None, None),
            P("band", "sub", None),
            P("band", "sub", None),
            P("band", "sub"),
        ),
        out_specs=P(None, ("band", "sub")),
        check_vma=False,
    )
```

```python
import jax
import jax.numpy as jnp
from jax import lax
from jax.experimental import pallas as pl
from jax.experimental.pallas import tpu as pltpu
from jax.sharding import PartitionSpec as P

OB_DEV = 8
PLANE = 32
OUTER = 64
LANES = 128
GROUP = 8
VMEM = pl.BlockSpec(memory_space=pltpu.VMEM)
SMEM = pl.BlockSpec(memory_space=pltpu.SMEM)
HBM = pl.BlockSpec(memory_space=pltpu.HBM)


def hbm(array):
    return pltpu.with_memory_space_constraint(array, pltpu.HBM)


def swap_pairs(count, first):
    pairs = []
    for i in range(first, count - 1, 2):
        pairs += [(i, i + 1), (i + 1, i)]
    return pairs


def xor_pairs(count, mask):
    return [(i, i ^ mask) for i in range(count)]


def index_copies(refs, scratch, sems):
    return [pltpu.make_async_copy(ref, to, sems.at[i]) for i, (ref, to) in enumerate(zip(refs, scratch))]


def entry(row_ref, code_ref, e, live):
    core, along = lax.axis_index("sub") % 2, lax.axis_index("sub") // 2
    code = code_ref[0, 0, e]
    dest = code // 16
    slot = ((dest % 2) ^ core) * 64 + ((dest // 2) ^ along) * 16 + code % 16
    return row_ref[0, 0, e], jnp.where(e < live, slot, 128)


def edge_rows(w_ref, e, width, right_first):
    right = w_ref[e, 2 * width - 16 : 2 * width, :].astype(jnp.float32)[15:16]
    left = w_ref[e, width : width + 16, :].astype(jnp.float32)[0:1]
    return jnp.where(right_first, right, left), jnp.where(right_first, left, right)


def column_block(rows, last, offset):
    place = lax.broadcasted_iota(jnp.int32, rows[0].shape, 1)
    block = jnp.zeros_like(rows[0])
    for r, values in enumerate(rows):
        block = jnp.where(place == offset + r, jnp.where(last, values[:, -1:], values[:, 0:1]), block)
    return block


def inner_kernel(
    row_hbm, code_hbm, live_ref, x_hbm, w_hbm, acc_ref, w_ref, meta_ref,
    row_ref, code_ref, row_lanes, code_lanes, x_ref, xf, source, edge, index_sems, x_sem, sems,
):
    fields, rows, width = x_ref.shape
    flat = fields * rows
    capacity = w_ref.shape[0]
    core, along = lax.axis_index("sub") % 2, lax.axis_index("sub") // 2
    indices = index_copies(
        (row_hbm, code_hbm, row_hbm, code_hbm), (row_ref, code_ref, row_lanes, code_lanes), index_sems
    )
    x_copy = pltpu.make_async_copy(x_hbm, x_ref, x_sem)

    def load(start):
        span = pl.ds(start, GROUP)
        return pltpu.make_async_copy(w_hbm.at[span], w_ref.at[span], sems.at[start // GROUP])

    live = live_ref[0, 0]
    for copy in indices:
        copy.start()
    x_copy.start()
    load(0).start()
    for start in range(GROUP, capacity, GROUP):
        pl.when(start < live)(lambda start=start: load(start).start())
    acc_ref[...] = jnp.zeros_like(acc_ref)
    edge[...] = jnp.zeros_like(edge)
    for copy in indices:
        copy.wait()
    x_copy.wait()
    x = x_ref[...].astype(jnp.float32).reshape(flat, width)
    lane = lax.broadcasted_iota(jnp.int32, (flat, width), 1)
    later = pltpu.roll(jnp.where(lane == 0, 0.0, x), width - 1, 1)
    earlier = pltpu.roll(jnp.where(lane == width - 1, 0.0, x), 1, 1)
    xf[0, 0:flat] = x
    xf[1, 0:flat] = 0.5 * (later - earlier)

    def row(which, r):
        return xf[which, pl.ds(r, fields, stride=rows), :]

    for r in range(rows):
        up = row(0, r - 1) if r > 0 else 0.0
        down = row(0, r + 1) if r < rows - 1 else 0.0
        source[r, :, 0:width] = row(0, r).astype(jnp.bfloat16)
        source[r, :, width : 2 * width] = row(1, r).astype(jnp.bfloat16)
        source[r, :, 2 * width : 3 * width] = (0.5 * (down - up)).astype(jnp.bfloat16)

    def accumulate(start):
        load(start).wait()
        for e in range(start, start + GROUP):
            to_mate, to_side = edge_rows(w_ref, e, width, core == 0)
            edge[0, e : e + 1] = to_mate
            edge[1, e : e + 1] = to_side
        places = [entry(row_ref, code_ref, e, live) for e in range(start, start + GROUP)]
        products = [
            jnp.dot(source[r], w_ref[start + i], preferred_element_type=jnp.float32) for i, (r, _) in enumerate(places)
        ]
        for (_, slot), product in zip(places, products):
            acc_ref[slot] += product

    accumulate(0)
    for start in range(GROUP, capacity, GROUP):
        pl.when(start < live)(lambda start=start: accumulate(start))
    meta_ref[0] = edge[0].astype(jnp.bfloat16)
    meta_ref[3] = edge[1].astype(jnp.bfloat16)
    columns = [row(0, r) for r in range(rows)]
    meta_ref[1] = column_block(columns, core == 0, 0).astype(jnp.bfloat16)
    meta_ref[4] = column_block(columns, core == 1, OUTER + core * rows).astype(jnp.bfloat16)
    code = code_lanes[0]
    dest = code // 16
    slot = ((dest % 2) ^ core) * 64 + ((dest // 2) ^ along) * 16 + code % 16
    alive = lax.broadcasted_iota(jnp.int32, slot.shape, 1) < live
    slot = jnp.where(alive, slot, 128)
    code = jnp.where(alive, code, 255)
    edge[0] = jnp.zeros_like(edge[0])
    edge[0, 0:1, 0:capacity] = row_lanes[0].astype(jnp.float32)
    edge[0, 1:2, 0:capacity] = slot.astype(jnp.float32)
    edge[0, 2:3, 0:capacity] = code.astype(jnp.float32)
    meta_ref[2] = edge[0].astype(jnp.bfloat16)


def border_kernel(
    row_hbm, code_hbm, live_ref, far_ref, first_ref, near_ref, w_ref, meta_ref, acc_in, acc_ref, send_ref,
    row_ref, code_ref, xf, ends, index_sems,
):
    del acc_in
    fields, rows, width = near_ref.shape
    flat = fields * rows
    capacity = w_ref.shape[0]
    indices = index_copies((row_hbm, code_hbm), (row_ref, code_ref), index_sems)
    for copy in indices:
        copy.start()
    odd_band = lax.axis_index("band") % 2 == 1
    near, first, far = (
        ref[...].astype(jnp.float32).reshape(flat, width) for ref in (near_ref, first_ref, far_ref)
    )
    near = near + first
    xf[0, 0:flat] = -0.5 * jnp.where(odd_band, near, far)
    xf[1, 0:flat] = 0.5 * jnp.where(odd_band, far, near)
    ends[...] = jnp.zeros_like(ends)
    ends[0] = xf[0, pl.ds(rows - 1, fields, stride=rows), :].astype(jnp.bfloat16)
    ends[rows - 1] = xf[1, pl.ds(0, fields, stride=rows), :].astype(jnp.bfloat16)
    for copy in indices:
        copy.wait()
    live = live_ref[0, 0]

    def accumulate(start):
        places = [entry(row_ref, code_ref, e, live) for e in range(start, start + GROUP)]
        products = [
            jnp.dot(ends[r], w_ref[start + i, 2 * width : 3 * width, :], preferred_element_type=jnp.float32)
            for i, (r, _) in enumerate(places)
        ]
        for (_, slot), product in zip(places, products):
            acc_ref[slot] += product

    accumulate(0)
    for start in range(GROUP, capacity, GROUP):
        pl.when(start < live)(lambda start=start: accumulate(start))
    extra = meta_ref.shape[0]
    half = send_ref.shape[0] - extra
    send_ref[0:half] = acc_ref[half : 2 * half].astype(jnp.bfloat16)
    send_ref[half : half + extra] = meta_ref[...]


def pair_sum_kernel(keep_ref, sent_ref, got_ref, own_ref, out_ref, select, edges):
    core, along = lax.axis_index("sub") % 2, lax.axis_index("sub") // 2
    count, fields, width = own_ref.shape
    chips = out_ref.shape[0]
    half = chips * count
    lane = lax.broadcasted_iota(jnp.int32, (1, width), 1)
    mine, theirs = sent_ref[half + 2].astype(jnp.float32), got_ref[half + 2].astype(jnp.float32)
    rolled = pltpu.roll(theirs, fields, 1)
    rows = jnp.where(lane < fields, mine[0:1], rolled[0:1])
    slots = jnp.where(lane < fields, mine[1:2], rolled[1:2] - half)
    place = lax.broadcasted_iota(jnp.int32, (width, width), 0).astype(jnp.float32)
    part = lax.broadcasted_iota(jnp.int32, (width, width), 1) // fields
    sign = jnp.where(core == 0, 0.5, -0.5)
    columns = jnp.zeros((fields, width), jnp.float32)
    for k, (block, factor) in enumerate(zip((got_ref[half + 1], sent_ref[half + 1]), (sign, -sign))):
        pick = jnp.where((place == rows) & (part == k), factor, 0.0).astype(jnp.bfloat16)
        columns = columns + jnp.dot(block, pick, preferred_element_type=jnp.float32)
    for t in range(half):
        select[t * fields : (t + 1) * fields] = jnp.where(slots == t, columns, 0.0).astype(jnp.bfloat16)
    edges[...] = jnp.zeros_like(edges)
    edges[0:fields] = sent_ref[half]
    edges[fields : 2 * fields] = got_ref[half]
    for k in range(chips):
        span = slice(k * count, (k + 1) * count)
        border = jnp.dot(
            select[k * count * fields : (k + 1) * count * fields], edges[...], preferred_element_type=jnp.float32
        )
        total = keep_ref[span] + got_ref[span].astype(jnp.float32) + border.reshape(count, fields, width)
        if k == 0:
            own_ref[...] = total
        out_ref[along ^ k, 0:count] = total.astype(jnp.bfloat16)
    first = core == 0
    outer = sent_ref[half + 4] + got_ref[half + 4]
    vectors = jnp.where(
        lax.broadcasted_iota(jnp.int32, mine.shape, 0) < 8,
        jnp.where(first, mine, theirs),
        pltpu.roll(jnp.where(first, theirs, mine), 8, 0),
    ).astype(jnp.bfloat16) + outer
    sides = [jnp.where(first == (k == 0), sent_ref[half + 3], got_ref[half + 3]) for k in range(2)]
    for k in range(chips):
        for i, block in enumerate((*sides, vectors)):
            out_ref[k, count + i] = block


def total_kernel(own_ref, got_ref, here_ref, next_ref, select, edges):
    sub = lax.axis_index("sub")
    along = sub // 2
    count, fields, width = own_ref.shape
    chips, rows = got_ref.shape[0], 8
    sets = width // fields
    lane = lax.broadcasted_iota(jnp.int32, (1, width), 1)
    place = lax.broadcasted_iota(jnp.int32, (width, width), 0).astype(jnp.float32)
    total = own_ref[...]
    for k in range(1, chips):
        total = total + got_ref[along ^ k, 0:count].astype(jnp.float32)
    for group in range(2 * chips // sets):
        columns = jnp.zeros((fields, width), jnp.float32)
        targets = jnp.full((1, width), -1.0, jnp.float32)
        for i in range(sets):
            chip, core = divmod(group * sets + i, 2)
            edges[group, i * fields : (i + 1) * fields] = got_ref[chip, count + core]
            vectors = got_ref[chip, count + 2].astype(jnp.float32)
            if i:
                vectors = pltpu.roll(vectors, i * fields, 1)
            inside = (lane >= i * fields) & (lane < (i + 1) * fields)
            targets = jnp.where(inside, vectors[8 * core + 2 : 8 * core + 3], targets)
            beside = chip + 2 * core - 1
            if 0 <= beside < chips:
                source = vectors[8 * core : 8 * core + 1] + (OUTER if core else OUTER + rows)
                pick = jnp.where((place == source) & inside, 0.5 if core else -0.5, 0.0).astype(jnp.bfloat16)
                columns = columns + jnp.dot(got_ref[beside, count + 2], pick, preferred_element_type=jnp.float32)
        targets = targets - (sub * count).astype(jnp.float32)
        for t in range(count):
            select[t * fields : (t + 1) * fields] = jnp.where(targets == t, columns, 0.0).astype(jnp.bfloat16)
        border = jnp.dot(select[...], edges[group], preferred_element_type=jnp.float32)
        total = total + border.reshape(count, fields, width)
    here_ref[...] = total[:OB_DEV]
    next_ref[...] = total[OB_DEV:].astype(jnp.bfloat16)


def final_kernel(here_ref, got_ref, out_ref):
    for q in range(OB_DEV):
        out_ref[:, q * LANES : (q + 1) * LANES] = here_ref[q] + got_ref[q].astype(jnp.float32)


def shards(atmos_flux, weight_tiles, source_row, target_code, live_count):
    fields, rows, width = atmos_flux.shape
    capacity = weight_tiles.shape[2]
    subs, bands = lax.axis_size("sub"), lax.axis_size("band")
    blocks = 2 * OB_DEV
    half = subs // 2 * blocks
    params = pltpu.CompilerParams(vmem_limit_bytes=24 * 2**20)
    far = lax.ppermute(atmos_flux, "band", swap_pairs(bands, 1))
    pairs = swap_pairs(bands, 0)
    first = lax.ppermute(atmos_flux, "band", [p for p in pairs if min(p) % PLANE == 0])
    near = lax.ppermute(atmos_flux, "band", [p for p in pairs if min(p) % PLANE != 0])
    sums = jax.ShapeDtypeStruct((2 * half + 1, fields, width), jnp.float32)
    indices = (hbm(source_row), hbm(target_code))
    index_scratch = [pltpu.SMEM(a.shape, a.dtype) for a in indices]
    tiles = hbm(weight_tiles[0, 0])
    meta = jax.ShapeDtypeStruct((5, fields, width), jnp.bfloat16)
    acc, held, meta = pl.pallas_call(
        inner_kernel,
        out_shape=(sums, jax.ShapeDtypeStruct(tiles.shape, tiles.dtype), meta),
        in_specs=[HBM, HBM, SMEM, HBM, HBM],
        out_specs=(VMEM, VMEM, VMEM),
        scratch_shapes=index_scratch + [pltpu.VMEM(a.shape, a.dtype) for a in indices] + [
            pltpu.VMEM((fields, rows, width), atmos_flux.dtype),
            pltpu.VMEM((2, fields * rows + rows, width), jnp.float32),
            pltpu.VMEM((rows, fields, 3 * width), jnp.bfloat16),
            pltpu.VMEM((2, capacity, width), jnp.float32),
            pltpu.SemaphoreType.DMA((4,)),
            pltpu.SemaphoreType.DMA,
            pltpu.SemaphoreType.DMA((capacity // GROUP,)),
        ],
        compiler_params=params,
        cost_estimate=pl.CostEstimate(flops=100_000_000, bytes_accessed=6_000_000, transcendentals=0),
        name="inner",
    )(*indices, live_count, hbm(atmos_flux), tiles)
    payload = jax.ShapeDtypeStruct((half + 5, fields, width), jnp.bfloat16)
    acc, send = pl.pallas_call(
        border_kernel,
        out_shape=(sums, payload),
        in_specs=[HBM, HBM, SMEM] + [VMEM] * 6,
        out_specs=(VMEM, VMEM),
        scratch_shapes=index_scratch + [
            pltpu.VMEM((2, fields * rows + rows, width), jnp.float32),
            pltpu.VMEM((rows, fields, width), jnp.bfloat16),
            pltpu.SemaphoreType.DMA((2,)),
        ],
        input_output_aliases={8: 0},
        compiler_params=params,
        cost_estimate=pl.CostEstimate(flops=30_000_000, bytes_accessed=4_000_000, transcendentals=0),
        name="border",
    )(*indices, live_count, far, first, near, held, meta, acc)
    got = lax.ppermute(send, "sub", xor_pairs(subs, 1))
    own, outs = pl.pallas_call(
        pair_sum_kernel,
        out_shape=(
            jax.ShapeDtypeStruct((blocks, fields, width), jnp.float32),
            jax.ShapeDtypeStruct((subs // 2, blocks + 3, fields, width), jnp.bfloat16),
        ),
        in_specs=[VMEM] * 3,
        out_specs=(VMEM, VMEM),
        scratch_shapes=[
            pltpu.VMEM((half * fields, width), jnp.bfloat16),
            pltpu.VMEM((width, width), jnp.bfloat16),
        ],
        compiler_params=params,
        name="pair_sum",
    )(acc, send, got)
    groups = [list(range(core, subs, 2)) for core in range(2)]
    arrived = lax.all_to_all(outs, "sub", split_axis=0, concat_axis=0, axis_index_groups=groups, tiled=True)
    here, ahead = pl.pallas_call(
        total_kernel,
        out_shape=(
            jax.ShapeDtypeStruct((OB_DEV, fields, width), jnp.float32),
            jax.ShapeDtypeStruct((OB_DEV, fields, width), jnp.bfloat16),
        ),
        in_specs=[VMEM] * 2,
        out_specs=(VMEM, VMEM),
        scratch_shapes=[
            pltpu.VMEM((blocks * fields, width), jnp.bfloat16),
            pltpu.VMEM((subs * fields // width, width, width), jnp.bfloat16),
        ],
        compiler_params=params,
        name="total",
    )(own, arrived)
    behind = lax.ppermute(ahead, "band", [(i, (i + 1) % bands) for i in range(bands)])
    return pl.pallas_call(
        final_kernel,
        out_shape=jax.ShapeDtypeStruct((fields, OB_DEV * width), jnp.float32),
        in_specs=[VMEM] * 2,
        out_specs=VMEM,
        compiler_params=params,
        name="final",
    )(here, behind)


def solution(mesh):
    return jax.shard_map(
        shards,
        mesh=mesh,
        in_specs=(
            P(None, "band", "sub"),
            P("band", "sub", None, None, None),
            P("band", "sub", None),
            P("band", "sub", None),
            P("band", "sub"),
        ),
        out_specs=P(None, ("band", "sub")),
        check_vma=False,
    )
```
